32 devices in a mesh: dp: 8 (over z, y), seq: 4 (over x, core).
Axes of the slice: x: 2, y: 2, z: 4, core: 2. Of those that a mesh axis runs over, the one named last changes fastest.
Arguments:
- tokens: bfloat16 [24, 640, 1024], P('dp', 'seq'), may hold values from -6 to 6
- cotangent: bfloat16 [24, 640, 1024], P('dp', 'seq'), may hold values from -6 to 6
- token_mask: int32 [24, 640], P('dp'), may hold values from 0 to 1, as said below
- w_qkv: bfloat16 [1024, 3072], P(('dp', 'seq')), may hold values from -0.1875 to 0.1875
- w_out: bfloat16 [1024, 1024], P(('dp', 'seq')), may hold values from -1.5 to 1.5
- w_fc1: bfloat16 [1024, 4096], P(('dp', 'seq')), may hold values from -0.1875 to 0.1875
- w_fc2: bfloat16 [4096, 1024], P(('dp', 'seq')), may hold values from -0.09375 to 0.09375
- b_q: bfloat16 [1024], P(('dp', 'seq')), may hold values from -3 to 3
- b_v: bfloat16 [1024], P(('dp', 'seq')), may hold values from -3 to 3
- b_out: bfloat16 [1024], P(('dp', 'seq')), may hold values from -3 to 3
- b_fc1: bfloat16 [4096], P(('dp', 'seq')), may hold values from -3 to 3
- b_fc2: bfloat16 [1024], P(('dp', 'seq')), may hold values from -3 to 3
- ln1_gain: bfloat16 [1024], P(('dp', 'seq')), may hold values from 0.5 to 1.5
- ln1_shift: bfloat16 [1024], P(('dp', 'seq')), may hold values from -3 to 3
- ln2_gain: bfloat16 [1024], P(('dp', 'seq')), may hold values from 0.5 to 1.5
- ln2_shift: bfloat16 [1024], P(('dp', 'seq')), may hold values from -3 to 3
Outputs:
- out_tokens: bfloat16 [24, 640, 1024], P('dp', 'seq')
- grad_tokens: float32 [24, 640, 1024], P('dp', 'seq')
- grad_w_qkv: float32 [1024, 3072], P(('dp', 'seq'))
- grad_w_out: float32 [1024, 1024], P(('dp', 'seq'))
- grad_w_fc1: float32 [1024, 4096], P(('dp', 'seq'))
- grad_w_fc2: float32 [4096, 1024], P(('dp', 'seq'))
- grad_b_q: float32 [1024], P(('dp', 'seq'))
- grad_b_v: float32 [1024], P(('dp', 'seq'))
- grad_b_out: float32 [1024], P(('dp', 'seq'))
- grad_b_fc1: float32 [4096], P(('dp', 'seq'))
- grad_b_fc2: float32 [1024], P(('dp', 'seq'))
- grad_ln1_gain: float32 [1024], P(('dp', 'seq'))
- grad_ln1_shift: float32 [1024], P(('dp', 'seq'))
- grad_ln2_gain: float32 [1024], P(('dp', 'seq'))
- grad_ln2_shift: float32 [1024], P(('dp', 'seq'))
The draws below stay inside these ranges and needn't reach their ends.
Inputs may be any that keep to these rules, and one draw needn't show every extreme that they name: `token_mask`: every row is either all zeros (an empty slot) or holds exactly 577 ones at positions drawn anew for each image; each aligned block of 3 rows (the slots of one dp group) holds between (3 + 1) // 2 and 3 images, and some block holds 3.
All inputs are finite; a program needn't handle non-finite values.
Results may differ from the reference program's by a relative error of at most 0.013.
Values may be sent and summed in bfloat16 or wider, within the bound.
No kernel may reach another device: no remote copies, remote signals or barrier semaphores. Data moves between devices by JAX's collectives and lax.ppermute only.
A program may use at most 192 MiB of HBM per device.

```python
import math
import jax
import jax.numpy as jnp
from jax import lax

D = 1024
HEADS = 16
HEAD_DIM = 64
FF = 4096
LEN = 640
REAL = 577
SLOTS = 3
IMAGES = 24
N_DP = 8


def draw_token_mask(key, part):
    key = jax.random.fold_in(key, 7)
    key_count, key_full, key_slot, key_place = jax.random.split(key, 4)
    least = (SLOTS + 1) // 2
    counts = jax.random.randint(key_count, (N_DP,), least, SLOTS + 1)
    full_group = jax.random.randint(key_full, (), 0, N_DP)
    counts = jnp.where(jnp.arange(N_DP) == full_group, SLOTS, counts)
    slot_scores = jax.random.randint(key_slot, (N_DP, SLOTS), 0, 1 << 20) * SLOTS + jnp.arange(SLOTS)[None, :]
    slot_ranks = jnp.argsort(jnp.argsort(slot_scores, axis=1, stable=True), axis=1, stable=True)
    live = (slot_ranks < counts[:, None]).reshape(N_DP * SLOTS, 1)
    place_scores = jax.random.randint(key_place, (N_DP * SLOTS, LEN), 0, 1 << 16) * LEN + jnp.arange(LEN)[None, :]
    place_ranks = jnp.argsort(jnp.argsort(place_scores, axis=1, stable=True), axis=1, stable=True)
    real_tokens = place_ranks < REAL
    return jnp.logical_and(real_tokens, live).astype(jnp.int32)


def block_levels(rng, dims, pieces, smallest, top_value):
    level, own = 1.0, jax.random.fold_in(rng, 6)
    for position, shards_of in pieces:
        heights = jnp.exp(jax.random.uniform(jax.random.fold_in(own, position), (shards_of,), jnp.float32, smallest / len(pieces), top_value / len(pieces)))
        level = level * jnp.repeat(heights, dims[position] // shards_of).reshape([-1 if axis == position else 1 for axis in range(len(dims))])
    return level


def normal_values(stream_key, shape, scale, most, cuts=(), kind=jnp.bfloat16):
    values = jax.random.normal(stream_key, shape, jnp.float32) * scale
    if len(cuts) > 0:
        values = block_levels(stream_key, shape, cuts, -0.22, 0.18) * values
    return jnp.clip(values, min=-most, max=most).astype(kind)


def setup_inputs(seed: int = 0) -> dict:
    arg_keys = jax.random.split(jax.random.key(seed), 17)
    tokens = normal_values(arg_keys[0], (IMAGES, LEN, D), 1.0, 6.0, ((0, 8), (1, 4)))
    cotangent = normal_values(arg_keys[1], (IMAGES, LEN, D), 1.0, 6.0, ((0, 8), (1, 4)))
    token_mask = draw_token_mask(jax.random.fold_in(arg_keys[16], 71), 0)
    w_qkv = normal_values(arg_keys[3], (D, 3 * D), D ** -0.5, 0.1875, ((0, 32),))
    w_out = normal_values(arg_keys[4], (D, D), (D // 64) ** -0.5, 1.5, ((0, 32),))
    w_fc1 = normal_values(arg_keys[5], (D, FF), D ** -0.5, 0.1875, ((0, 32),))
    w_fc2 = normal_values(arg_keys[6], (FF, D), FF ** -0.5, 0.09375, ((0, 32),))
    b_q = normal_values(arg_keys[7], (D,), 0.3, 3.0, ((0, 32),))
    b_v = normal_values(arg_keys[8], (D,), 0.3, 3.0, ((0, 32),))
    b_out = normal_values(arg_keys[9], (D,), 0.3, 3.0, ((0, 32),))
    b_fc1 = normal_values(arg_keys[10], (FF,), 0.3, 3.0, ((0, 32),))
    b_fc2 = normal_values(arg_keys[11], (D,), 0.3, 3.0, ((0, 32),))
    ln1_gain = jnp.clip(1.0 + 0.1 * jax.random.normal(arg_keys[12], (D,), jnp.float32), 0.5, 1.5).astype(jnp.bfloat16)
    ln1_shift = normal_values(arg_keys[13], (D,), 0.3, 3.0, ((0, 32),))
    ln2_gain = jnp.clip(1.0 + 0.1 * jax.random.normal(arg_keys[14], (D,), jnp.float32), 0.5, 1.5).astype(jnp.bfloat16)
    ln2_shift = normal_values(arg_keys[15], (D,), 0.3, 3.0, ((0, 32),))
    return {"tokens": tokens, "cotangent": cotangent, "token_mask": token_mask, "w_qkv": w_qkv, "w_out": w_out, "w_fc1": w_fc1, "w_fc2": w_fc2, "b_q": b_q, "b_v": b_v, "b_out": b_out, "b_fc1": b_fc1, "b_fc2": b_fc2, "ln1_gain": ln1_gain, "ln1_shift": ln1_shift, "ln2_gain": ln2_gain, "ln2_shift": ln2_shift}


EPS = 1e-06

@jax.custom_vjp
def low(v):
    return lax.optimization_barrier(v.astype(jnp.bfloat16)).astype(jnp.float32)

@jax.custom_vjp
def low_back(v):
    return v

def low_keep(v):
    return (low(v), None)

def low_pass(kept, grad):
    return (grad,)

def back_keep(v):
    return (v, None)

def back_low(kept, grad):
    return (low(grad),)
low.defvjp(low_keep, low_pass)
low_back.defvjp(back_keep, back_low)

def layer_norm(values, gain, shift):
    average = lax.optimization_barrier(jnp.mean(values, axis=-1, keepdims=True))
    centred = values - average
    spread = lax.optimization_barrier(jnp.mean(centred * centred, axis=-1, keepdims=True))
    return centred * lax.rsqrt(spread + EPS) * gain + shift

def product(left, right):
    return jnp.dot(left, right, precision=lax.Precision.HIGHEST)

def attend(item):
    queries, keys, values, keep = item
    scale_factor = 1.0 / math.sqrt(HEAD_DIM)
    q_heads = queries.reshape(LEN, HEADS, HEAD_DIM)
    k_heads = keys.reshape(LEN, HEADS, HEAD_DIM)
    v_heads = values.reshape(LEN, HEADS, HEAD_DIM)
    scores = low_back(jnp.einsum('qhd,khd->hqk', q_heads, k_heads, precision=lax.Precision.HIGHEST) * scale_factor)
    masked = jnp.where(keep[None, None, :], scores, -1000000000.0)
    largest = lax.optimization_barrier(jnp.max(masked, axis=-1, keepdims=True))
    raised = jnp.exp(masked - largest)
    chance = low(raised / lax.optimization_barrier(jnp.sum(raised, axis=-1, keepdims=True)))
    mixed = jnp.einsum('hqk,khd->qhd', chance, v_heads, precision=lax.Precision.HIGHEST)
    return mixed.reshape(LEN, D)

def block(inputs, mask, params):
    w_qkv, w_out, w_fc1, w_fc2, b_q, b_v, b_out, b_fc1, b_fc2, ln1_gain, ln1_shift, ln2_gain, ln2_shift = params
    rows = inputs.reshape(-1, D)
    keep = mask > 0
    valid = keep.reshape(-1, 1).astype(jnp.float32)
    normed = low(layer_norm(rows, ln1_gain, ln1_shift))
    qkv_bias = jnp.concatenate([b_q, jnp.zeros_like(b_out), b_v])
    projected = low(low_back(product(normed, w_qkv) + qkv_bias))
    queries = projected[:, :D].reshape(SLOTS, LEN, D)
    keys = projected[:, D:2 * D].reshape(SLOTS, LEN, D)
    values = projected[:, 2 * D:].reshape(SLOTS, LEN, D)
    attended = lax.map(jax.checkpoint(attend), (queries, keys, values, keep))
    attended = low(low_back(attended.reshape(-1, D)))
    branch = low_back(product(attended, w_out) + b_out)
    middle = rows + branch
    second = low(layer_norm(middle, ln2_gain, ln2_shift))
    hidden = low_back(product(second, w_fc1) + b_fc1)
    activated = low(jax.nn.gelu(hidden, approximate=False))
    out_branch = low_back(product(activated, w_fc2) + b_fc2)
    return (middle + out_branch) * valid

def reference(tokens, cotangent, token_mask, w_qkv, w_out, w_fc1, w_fc2, b_q, b_v, b_out, b_fc1, b_fc2, ln1_gain, ln1_shift, ln2_gain, ln2_shift):
    params = tuple((weight.astype(jnp.float32) for weight in (w_qkv, w_out, w_fc1, w_fc2, b_q, b_v, b_out, b_fc1, b_fc2, ln1_gain, ln1_shift, ln2_gain, ln2_shift)))
    group_inputs = tokens.astype(jnp.float32).reshape(N_DP, SLOTS, LEN, D)
    group_cots = cotangent.astype(jnp.float32).reshape(N_DP, SLOTS * LEN, D)
    group_masks = token_mask.reshape(N_DP, SLOTS, LEN)

    def step(running, item):
        group_tokens, group_cot, group_mask = item

        def forward(inputs, weights):
            return block(inputs, group_mask, weights)
        result, pull = jax.vjp(forward, group_tokens, params)
        grad_inputs, grad_params = pull(group_cot)
        running = jax.tree.map(lambda left, right: left + right, running, grad_params)
        return (running, (result.astype(jnp.bfloat16), grad_inputs.reshape(SLOTS, LEN, D)))
    zeros = tuple((jnp.zeros_like(weight) for weight in params))
    running, (results, grads) = lax.scan(step, zeros, (group_inputs, group_cots, group_masks))
    out_tokens = results.reshape(IMAGES, LEN, D)
    grad_tokens = grads.reshape(IMAGES, LEN, D)
    return (out_tokens, grad_tokens, running[0], running[1], running[2], running[3], running[4], running[5], running[6], running[7], running[8], running[9], running[10], running[11], running[12])
```

```python
import math

import jax
import jax.numpy as jnp
from jax import lax
from jax.experimental import pallas as pl
from jax.experimental.pallas import tpu as pltpu
from jax.sharding import PartitionSpec as P

HEAD_DIM = 64
PAIR = 2 * HEAD_DIM
EPS = 1e-06
MASKED = -1000000000.0
SCALE = 1.0 / math.sqrt(HEAD_DIM)
F32 = jnp.float32
BF16 = jnp.bfloat16
QUICK = pl.CostEstimate(flops=0, bytes_accessed=0, transcendentals=0)


def after(values, *others):
    return lax.optimization_barrier((values, others))[0]


class Grid:
    def __init__(self):
        self.dp, self.seq = lax.axis_size("dp"), lax.axis_size("seq")
        self.depth = self.dp // 2
        place, spot = lax.axis_index("dp"), lax.axis_index("seq")
        self.z, self.y = place // 2, place % 2
        self.x, self.core = spot // 2, spot % 2

    def over_core(self, values):
        return lax.ppermute(values, "seq", [(i, i ^ 1) for i in range(self.seq)])

    def over_x(self, values):
        return lax.ppermute(values, "seq", [(i, i ^ 2) for i in range(self.seq)])

    def over_y(self, values):
        return lax.ppermute(values, "dp", [(i, i ^ 1) for i in range(self.dp)])

    def along_z(self, values, step):
        return lax.ppermute(values, "dp", [(i, (i + 2 * step) % self.dp) for i in range(self.dp)])


def pick(values, index, axis):
    return lax.dynamic_index_in_dim(values, index, axis, keepdims=False)


def add(left, right):
    return (left.astype(F32) + right.astype(F32)).astype(left.dtype)


def gather_z(grid, *shards):
    columns = []
    for shard in shards:
        column = [shard]
        for _ in range(1, grid.depth):
            column.append(grid.along_z(column[-1], 1))
        columns.append(column)
    return jnp.stack([jnp.concatenate(parts, axis=1) for parts in zip(*columns)])


def gather_near(grid, column):
    return grid.over_x(column), grid.over_y(column)


def gather_far(grid, by_x, by_y):
    half = grid.depth // 2
    return grid.over_y(by_x[:half]), grid.over_x(by_y[half:])


def assemble(grid, widths, column, near, far):
    parts = []
    half = grid.depth // 2
    for part, first, flip_x, flip_y in (
        (column, 0, 0, 0),
        (near[0], 0, 1, 0),
        (near[1], 0, 0, 1),
        (far[0], 0, 1, 1),
        (far[1], half, 1, 1),
    ):
        parts.append((part, first, flip_x, flip_y, 0))
        parts.append((grid.over_core(part), first, flip_x, flip_y, 1))
    places = [where[1:] for where in parts]
    parts = [part for part, *_ in parts]
    depth, rows, _ = column.shape
    if rows % 16 == 0:
        wholes = assemble_by_copies(depth, places, widths, parts)
    else:
        whole = jnp.zeros((depth, 2, 2, 2) + column.shape[1:], column.dtype)
        for part, (first, flip_x, flip_y, flip_core) in zip(parts, places):
            for k in range(part.shape[0]):
                where = ((grid.z - first - k) % depth, grid.y ^ flip_y, grid.x ^ flip_x, grid.core ^ flip_core)
                whole = lax.dynamic_update_slice(whole, part[k][None, None, None, None], where + (0, 0))
        starts = [sum(widths[:i]) for i in range(len(widths))]
        wholes = [whole[..., start : start + width] for start, width in zip(starts, widths)]
    return [whole.reshape(-1, width) for whole, width in zip(wholes, widths)]


def assemble_by_copies(depth, places, widths, parts):
    rows, wide = parts[0].shape[1:]
    blocks = sum(part.shape[0] for part in parts)
    starts = [sum(widths[:i]) for i in range(len(widths))]

    def kernel(*refs):
        sources, targets = refs[: len(parts)], refs[len(parts) : -3]
        held, came, went = refs[-3:]
        place, spot = lax.axis_index("dp"), lax.axis_index("seq")
        z, y, x, core = place // 2, place % 2, spot // 2, spot % 2
        steps = []
        for source, (first, flip_x, flip_y, flip_core) in zip(sources, places):
            across_y = 1 - y if flip_y else y
            across_x = 1 - x if flip_x else x
            across_core = 1 - core if flip_core else core
            for k in range(source.shape[0]):
                height = lax.rem(z + (2 * depth - first - k), depth)
                slot = len(steps)
                read = pltpu.make_async_copy(source.at[k], held.at[slot], came.at[slot])
                read.start()
                steps.append((read, (height, across_y, across_x, across_core)))
        writes = []
        for slot, (read, where) in enumerate(steps):
            read.wait()
            for i, target in enumerate(targets):
                write = pltpu.make_async_copy(
                    held.at[slot, :, starts[i] : starts[i] + widths[i]],
                    target.at[where],
                    went.at[slot, i],
                )
                write.start()
                writes.append(write)
        for write in writes:
            write.wait()

    shapes = [jax.ShapeDtypeStruct((depth, 2, 2, 2, rows, width), parts[0].dtype) for width in widths]
    return pl.pallas_call(
        kernel,
        in_specs=[pl.BlockSpec(memory_space=pl.ANY)] * len(parts),
        out_specs=[pl.BlockSpec(memory_space=pl.ANY)] * len(widths),
        out_shape=shapes,
        scratch_shapes=[
            pltpu.VMEM((blocks, rows, wide), parts[0].dtype),
            pltpu.SemaphoreType.DMA((blocks,)),
            pltpu.SemaphoreType.DMA((blocks, len(widths))),
        ],
        compiler_params=pltpu.CompilerParams(vmem_limit_bytes=32 * 2**20),
        cost_estimate=pl.CostEstimate(
            flops=0, bytes_accessed=4 * sum(part.size for part in parts), transcendentals=0
        ),
        name="assemble",
    )(*parts)


def reduce_core(grid, terms):
    terms = terms.reshape(grid.depth, 2, 2, 2, -1, terms.shape[-1])
    return add(pick(terms, grid.core, 3), grid.over_core(pick(terms, 1 - grid.core, 3)))


def block_at(total, y, x):
    return pick(pick(total, y, 1), x, 1)


def reduce_far(grid, total, by_x):
    part = grid.depth * by_x // 4
    far = block_at(total, 1 - grid.y, 1 - grid.x)
    return (grid.over_x(far[:part]) if part else None), grid.over_y(far[part:])


def reduce_near(grid, total, far):
    from_x, from_y = far
    to_x = block_at(total, grid.y, 1 - grid.x)
    to_y = block_at(total, 1 - grid.y, grid.x)
    part = 0 if from_x is None else from_x.shape[0]
    to_x = jnp.concatenate([to_x[:part], add(to_x[part:], from_y)])
    if part:
        to_y = jnp.concatenate([add(to_y[:part], from_x), to_y[part:]])
    return grid.over_x(to_x), grid.over_y(to_y)


def reduce_z(grid, total, near):
    own = block_at(total, grid.y, grid.x).astype(F32) + near[0].astype(F32) + near[1].astype(F32)
    low = own.astype(total.dtype)
    result = pick(own, grid.z, 0)
    for step in range(1, grid.depth):
        sent = pick(low, (grid.z + step) % grid.depth, 0)
        result = result + grid.along_z(sent, step).astype(F32)
    return result


def reduce_small(grid, terms):
    total = terms.reshape((grid.depth, 2, 2, 2) + terms.shape[1:])
    total = pick(total, grid.core, 3) + grid.over_core(pick(total, 1 - grid.core, 3))
    total = pick(total, grid.x, 2) + grid.over_x(pick(total, 1 - grid.x, 2))
    total = pick(total, grid.y, 1) + grid.over_y(pick(total, 1 - grid.y, 1))
    result = pick(total, grid.z, 0)
    for step in range(1, grid.depth):
        result = result + grid.along_z(pick(total, (grid.z + step) % grid.depth, 0), step)
    return result


def dot_rows(left, right):
    return lax.dot_general(left, right, (((1,), (1,)), ((), ())), preferred_element_type=F32)


def dot_columns(left, right):
    return lax.dot_general(left, right, (((0,), (0,)), ((), ())), preferred_element_type=F32)


def attend_forward_kernel(keep_ref, q_ref, k_ref, v_ref, out_ref, log_ref):
    keep = keep_ref[0] > 0
    queries = q_ref[0, 0]
    keys = k_ref[:, 0].reshape(-1, PAIR)
    values = v_ref[:, 0].reshape(-1, PAIR)
    outs, logs = [], []
    for head in range(2):
        part = slice(head * HEAD_DIM, (head + 1) * HEAD_DIM)
        scores = dot_rows(queries[:, part] * SCALE, keys[:, part])
        scores = jnp.where(keep, scores, MASKED)
        largest = jnp.max(scores, axis=-1, keepdims=True)
        raised = jnp.exp(scores - largest)
        totals = jnp.sum(raised, axis=-1, keepdims=True)
        mixed = jnp.dot(raised.astype(BF16), values[:, part], preferred_element_type=F32)
        outs.append(mixed / totals)
        logs.append(largest + jnp.log(totals))
    out_ref[0] = jnp.concatenate(outs, axis=1).astype(BF16)
    log_ref[0, 0] = jnp.concatenate(logs, axis=1)


def attend_forward(slot, projected, keep):
    blocks, _, local_len, wide = projected.shape
    width = wide // 3
    pairs = width // PAIR
    full_len = blocks * local_len
    return pl.pallas_call(
        attend_forward_kernel,
        grid=(pairs,),
        in_specs=[
            pl.BlockSpec((1, 1, full_len), lambda p: (slot, 0, 0)),
            pl.BlockSpec((1, 1, local_len, PAIR), lambda p: (0, slot, 0, p)),
            pl.BlockSpec((blocks, 1, local_len, PAIR), lambda p: (0, slot, 0, pairs + p)),
            pl.BlockSpec((blocks, 1, local_len, PAIR), lambda p: (0, slot, 0, 2 * pairs + p)),
        ],
        out_specs=[
            pl.BlockSpec((1, local_len, PAIR), lambda p: (0, 0, p)),
            pl.BlockSpec((1, 1, local_len, 2), lambda p: (0, p, 0, 0)),
        ],
        out_shape=[
            jax.ShapeDtypeStruct((1, local_len, width), BF16),
            jax.ShapeDtypeStruct((1, pairs, local_len, 2), F32),
        ],
        cost_estimate=QUICK,
        compiler_params=pltpu.CompilerParams(vmem_limit_bytes=32 * 2**20),
        name="attend_forward",
    )(keep, projected, projected, projected)


def attend_backward_kernel(keep_ref, q_ref, k_ref, v_ref, log_ref, g_ref, dq_ref, own_ref, send_ref):
    keep = keep_ref[0] > 0
    blocks, _, local_len, _ = k_ref.shape
    queries = q_ref[0, 0]
    keys = k_ref[:, 0].reshape(-1, PAIR)
    values = v_ref[:, 0].reshape(-1, PAIR)
    grads = g_ref[0]
    logs = log_ref[0, 0]
    dqs, dks, dvs = [], [], []
    for head in range(2):
        part = slice(head * HEAD_DIM, (head + 1) * HEAD_DIM)
        scaled = queries[:, part] * SCALE
        scores = jnp.where(keep, dot_rows(scaled, keys[:, part]), MASKED)
        chance = jnp.exp(scores - logs[:, head : head + 1])
        grad_chance = dot_rows(grads[:, part], values[:, part])
        product = chance * grad_chance
        inner = jnp.sum(product, axis=-1, keepdims=True)
        grad_scores = jnp.where(keep, product - chance * inner, 0.0).astype(BF16)
        dqs.append(jnp.dot(grad_scores, keys[:, part], preferred_element_type=F32) * SCALE)
        dks.append(dot_columns(scaled, grad_scores))
        dvs.append(dot_columns(grads[:, part], chance.astype(BF16)))
    dq_ref[0] = jnp.concatenate(dqs, axis=1).astype(BF16)
    for kind, terms in enumerate((dks, dvs)):
        turned = jnp.concatenate(terms, axis=0).T.astype(BF16).reshape(blocks, local_len, PAIR)
        for block in range(blocks):
            target = send_ref if block % 2 else own_ref
            target[block // 2, kind] = turned[block]


def attend_backward(slot, projected, keep, logs, grad_attended):
    blocks, slots, local_len, wide = projected.shape
    width = wide // 3
    pairs = width // PAIR
    full_len = blocks * local_len
    terms = jax.ShapeDtypeStruct((blocks // 2, 2, local_len, width), BF16)
    terms_spec = pl.BlockSpec((blocks // 2, 2, local_len, PAIR), lambda p: (0, 0, 0, p))
    return pl.pallas_call(
        attend_backward_kernel,
        grid=(pairs,),
        in_specs=[
            pl.BlockSpec((1, 1, full_len), lambda p: (slot, 0, 0)),
            pl.BlockSpec((1, 1, local_len, PAIR), lambda p: (0, slot, 0, p)),
            pl.BlockSpec((blocks, 1, local_len, PAIR), lambda p: (0, slot, 0, pairs + p)),
            pl.BlockSpec((blocks, 1, local_len, PAIR), lambda p: (0, slot, 0, 2 * pairs + p)),
            pl.BlockSpec((1, 1, local_len, 2), lambda p: (0, p, 0, 0)),
            pl.BlockSpec((1, local_len, PAIR), lambda p: (slot, 0, p)),
        ],
        out_specs=[pl.BlockSpec((1, local_len, PAIR), lambda p: (0, 0, p)), terms_spec, terms_spec],
        out_shape=[jax.ShapeDtypeStruct((1, local_len, width), BF16), terms, terms],
        cost_estimate=QUICK,
        compiler_params=pltpu.CompilerParams(vmem_limit_bytes=32 * 2**20),
        name="attend_backward",
    )(keep, projected, projected, projected, logs, grad_attended)


def normalise(values):
    average = jnp.mean(values, axis=-1, keepdims=True)
    centred = values - average
    spread = jnp.mean(centred * centred, axis=-1, keepdims=True)
    scale = lax.rsqrt(spread + EPS)
    return centred * scale, scale


def normalise_back(grad, gain, normal, scale):
    inward = grad * gain
    mean_in = jnp.mean(inward, axis=-1, keepdims=True)
    mean_normal = jnp.mean(inward * normal, axis=-1, keepdims=True)
    values = scale * (inward - mean_in - normal * mean_normal)
    return values, jnp.sum(grad * normal, axis=0), jnp.sum(grad, axis=0)


def split_vectors(table, lengths):
    pieces, offset = [], 0
    for length in lengths:
        pieces.append(table[:, offset : offset + length].reshape(-1))
        offset += length
    return pieces


LANES = 128


def fold(vectors, rows):
    groups, count = vectors.shape
    per_row = -(-count // rows)
    vectors = jnp.pad(vectors, ((0, 0), (0, per_row * rows - count)))
    return jnp.pad(vectors.reshape(groups * rows, per_row), ((0, 0), (0, LANES - per_row)))


def unfold(block, rows, count):
    per_row = -(-count // rows)
    return block[:, :per_row].reshape(-1, per_row * rows)[:, :count]


def shards(
    tokens,
    cotangent,
    token_mask,
    w_qkv,
    w_out,
    w_fc1,
    w_fc2,
    b_q,
    b_v,
    b_out,
    b_fc1,
    b_fc2,
    ln1_gain,
    ln1_shift,
    ln2_gain,
    ln2_shift,
):
    grid = Grid()
    groups = grid.dp * grid.seq
    slots, local_len, width = tokens.shape
    count = slots * local_len
    vector_shards = (b_q, b_v, b_out, b_fc1, b_fc2, ln1_gain, ln1_shift, ln2_gain, ln2_shift)
    lengths = [vector.shape[0] for vector in vector_shards]

    total_len = sum(lengths)
    depth_rows = w_qkv.shape[0]

    vectors = fold(jnp.concatenate(vector_shards)[None], depth_rows)
    column_one = gather_z(grid, w_qkv, vectors)
    by_core, by_x = grid.over_core(tokens), grid.over_x(tokens)
    column_one, by_x = lax.optimization_barrier((column_one, by_x))
    near_one = gather_near(grid, column_one)
    column_two = gather_z(grid, after(jnp.concatenate([w_out, w_fc1], axis=1), column_one, by_x))
    near_one = lax.optimization_barrier(near_one)
    far_one = gather_far(grid, *near_one)
    seen = jnp.stack([tokens, by_core, by_x, grid.over_core(by_x)])
    full_qkv, vectors = assemble(grid, (w_qkv.shape[1], LANES), column_one, near_one, far_one)
    column_two = after(column_two, far_one)
    near_two = gather_near(grid, column_two)
    column_three = gather_z(grid, after(w_fc2, column_two))
    near_two = lax.optimization_barrier(near_two)
    far_two = gather_far(grid, *near_two)

    vectors = unfold(vectors, depth_rows, total_len)
    vectors = [v.astype(F32) for v in split_vectors(vectors, lengths)]
    bias_q, bias_v, bias_out, bias_fc1, bias_fc2, gain_one, shift_one, gain_two, shift_two = vectors
    spot = lax.axis_index("seq")
    blocks = grid.seq
    mask_blocks = token_mask.reshape(slots, blocks, local_len)
    keep = jnp.stack([pick(mask_blocks, spot ^ block, 1) for block in range(blocks)], 1)
    valid = (keep[:, 0] > 0).reshape(-1, 1).astype(F32)
    keep = keep.reshape(slots, 1, -1)

    rows = tokens.reshape(-1, width).astype(F32)
    normal_seen, _ = normalise(seen.reshape(-1, width).astype(F32))
    normed_seen = lax.optimization_barrier((normal_seen * gain_one + shift_one).astype(BF16))
    normed_low = normed_seen[:count]
    qkv_bias = jnp.concatenate([bias_q, jnp.zeros_like(bias_out), bias_v])
    projected = (jnp.dot(normed_seen, full_qkv, preferred_element_type=F32) + qkv_bias).astype(BF16)
    projected = projected.reshape(blocks, slots, local_len, 3 * width)

    column_three = after(column_three, far_two, projected)
    near_three = gather_near(grid, column_three)
    full_out, full_fc1 = assemble(grid, (width, w_fc1.shape[1]), column_two, near_two, far_two)
    attended, logs = zip(*[attend_forward(slot, projected, keep) for slot in range(slots)])
    near_three = after(near_three, attended)
    far_three = gather_far(grid, *near_three)
    (full_fc2,) = assemble(grid, (width,), column_three, near_three, far_three)

    attended = jnp.concatenate(attended).reshape(-1, width)
    middle = rows + jnp.dot(attended, full_out, preferred_element_type=F32) + bias_out
    normal_two, scale_two = normalise(middle)
    second_low = (normal_two * gain_two + shift_two).astype(BF16)
    hidden = jnp.dot(second_low, full_fc1, preferred_element_type=F32) + bias_fc1
    below = 0.5 * (1.0 + lax.erf(hidden * math.sqrt(0.5)))
    density = jnp.exp(-0.5 * hidden * hidden) * (1.0 / math.sqrt(2.0 * math.pi))
    activated_low = (hidden * below).astype(BF16)
    slope = (below + hidden * density).astype(BF16)
    activated_low, slope = lax.optimization_barrier((activated_low, slope))

    grad_y_low = cotangent.reshape(-1, width) * valid.astype(BF16)
    grad_y = grad_y_low.astype(F32)
    terms_fc2 = dot_columns(activated_low, grad_y_low).astype(BF16)
    sum_fc2 = reduce_core(grid, terms_fc2)
    grad_y_next, full_fc2 = after((grad_y_low, full_fc2), terms_fc2)
    grad_hidden = (dot_rows(grad_y_next, full_fc2) * slope.astype(F32)).astype(BF16)
    grad_hidden, sum_fc2 = lax.optimization_barrier((grad_hidden, sum_fc2))
    far_fc2 = reduce_far(grid, sum_fc2, 2)
    result = (
        middle + jnp.dot(activated_low, full_fc2, preferred_element_type=F32) + bias_fc2
    ) * valid
    out_tokens = result.astype(BF16).reshape(slots, local_len, width)
    grad_b_fc2 = jnp.sum(grad_y, axis=0)
    terms_fc1 = dot_columns(second_low, grad_hidden).astype(BF16)
    grad_b_fc1 = jnp.sum(grad_hidden.astype(F32), axis=0)
    grad_second = dot_rows(after(grad_hidden, terms_fc1), full_fc1)
    grad_middle, grad_gain_two, grad_shift_two = normalise_back(
        grad_second, gain_two, normal_two, scale_two
    )
    grad_middle = grad_y + grad_middle
    grad_branch = after(grad_middle.astype(BF16), far_fc2)
    near_fc2 = reduce_near(grid, sum_fc2, far_fc2)
    grad_b_out = jnp.sum(grad_branch.astype(F32), axis=0)
    terms_out = dot_columns(attended, grad_branch).astype(BF16)
    sum_two = jnp.concatenate([reduce_core(grid, terms_out), reduce_core(grid, terms_fc1)], axis=-1)
    grad_attended = dot_rows(grad_branch, full_out).astype(BF16).reshape(slots, local_len, width)

    parts, ahead = [], sum_two
    for slot in range(slots):
        grad_attended = after(grad_attended, ahead)
        grad_queries, own, send = attend_backward(slot, projected, keep, logs[slot], grad_attended)
        came = grid.over_core(send)
        across = add(own[1], came[1])
        ahead = (grad_queries, across) if slot == 0 else (grad_queries, across, parts[-1][3])
        if slot == 0:
            near_fc2 = after(near_fc2, grad_queries)
            far_two = reduce_far(grid, after(sum_two, near_fc2), 0)
            grad_w_fc2 = reduce_z(grid, sum_fc2, near_fc2)
            ahead = (grad_queries,)
        else:
            ahead = (grad_queries, parts[-1][4])
        parts.append((grad_queries, own[0], came[0], grid.over_x(across), across))
    near_two = reduce_near(grid, sum_two, far_two)
    grad_two = reduce_z(grid, sum_two, near_two)
    grad_w_out, grad_w_fc1 = grad_two[:, :width], grad_two[:, width:]

    grad_queries = jnp.concatenate([part[0] for part in parts]).reshape(-1, width)
    terms_q = dot_columns(normed_low, grad_queries).astype(BF16)
    sum_q = reduce_core(grid, terms_q)
    far_q = reduce_far(grid, sum_q, 0)
    grad_keys_values = [
        (own.astype(F32) + came.astype(F32) + across.astype(F32)).astype(BF16)
        for _, own, came, across, _ in parts
    ]
    grad_keys, grad_values = [jnp.stack([part[kind] for part in grad_keys_values]) for kind in range(2)]
    grad_kv = jnp.concatenate([grad_keys, grad_values], axis=-1).reshape(-1, 2 * width)
    grad_kv, grad_w_fc2 = lax.optimization_barrier((grad_kv, grad_w_fc2))
    terms_kv = dot_columns(normed_low, grad_kv).astype(BF16)
    sum_kv = reduce_core(grid, terms_kv)
    far_kv = reduce_far(grid, sum_kv, 2)
    grad_qkv = after(jnp.concatenate([grad_queries, grad_kv], axis=-1), terms_kv)
    grad_normed = dot_rows(grad_qkv, full_qkv)
    grad_qkv_wide = jnp.sum(grad_qkv.astype(F32), axis=0)
    grad_b_q = grad_qkv_wide[:width]
    grad_b_v = grad_qkv_wide[2 * width :]
    normal_one, scale_one = normalise(rows)
    grad_rows, grad_gain_one, grad_shift_one = normalise_back(
        grad_normed, gain_one, normal_one, scale_one
    )
    grad_tokens = (grad_middle + grad_rows).reshape(slots, local_len, width)
    terms = (
        grad_b_q,
        grad_b_v,
        grad_b_out,
        grad_b_fc1,
        grad_b_fc2,
        grad_gain_one,
        grad_shift_one,
        grad_gain_two,
        grad_shift_two,
    )
    terms = jnp.concatenate([term.reshape(groups, -1) for term in terms], axis=-1)
    owned = split_vectors(reduce_small(grid, terms[:, None]).reshape(1, -1), lengths)
    near_q = reduce_near(grid, sum_q, far_q)
    near_kv = reduce_near(grid, sum_kv, far_kv)
    grad_w_qkv = jnp.concatenate([reduce_z(grid, sum_q, near_q), reduce_z(grid, sum_kv, near_kv)], axis=-1)
    return (out_tokens, grad_tokens, grad_w_qkv, grad_w_out, grad_w_fc1, grad_w_fc2, *owned)


def solution(mesh):
    spread = P(("dp", "seq"))
    row = P("dp", "seq", None)
    matrix = P(("dp", "seq"), None)
    in_specs = (row, row, P("dp", None)) + (matrix,) * 4 + (spread,) * 9
    out_specs = (row, row) + (matrix,) * 4 + (spread,) * 9
    return jax.shard_map(shards, mesh=mesh, in_specs=in_specs, out_specs=out_specs, check_vma=False)
```

```python
import math

import jax
import jax.numpy as jnp
from jax import lax
from jax.experimental import pallas as pl
from jax.experimental.pallas import tpu as pltpu
from jax.sharding import PartitionSpec as P

HEAD_DIM = 64
PAIR = 2 * HEAD_DIM
EPS = 1e-06
MASKED = -1000000000.0
SCALE = 1.0 / math.sqrt(HEAD_DIM)
F32 = jnp.float32
BF16 = jnp.bfloat16
QUICK = pl.CostEstimate(flops=0, bytes_accessed=0, transcendentals=0)


def after(values, *others):
    return lax.optimization_barrier((values, others))[0]


class Grid:
    def __init__(self):
        self.dp, self.seq = lax.axis_size("dp"), lax.axis_size("seq")
        self.depth = self.dp // 2
        place, spot = lax.axis_index("dp"), lax.axis_index("seq")
        self.z, self.y = place // 2, place % 2
        self.x, self.core = spot // 2, spot % 2

    def over_core(self, values):
        return lax.ppermute(values, "seq", [(i, i ^ 1) for i in range(self.seq)])

    def over_x(self, values):
        return lax.ppermute(values, "seq", [(i, i ^ 2) for i in range(self.seq)])

    def over_y(self, values):
        return lax.ppermute(values, "dp", [(i, i ^ 1) for i in range(self.dp)])

    def along_z(self, values, step):
        return lax.ppermute(values, "dp", [(i, (i + 2 * step) % self.dp) for i in range(self.dp)])


def pick(values, index, axis):
    return lax.dynamic_index_in_dim(values, index, axis, keepdims=False)


def add(left, right):
    return (left.astype(F32) + right.astype(F32)).astype(left.dtype)


def gather_z(grid, *shards):
    columns = []
    for shard in shards:
        column = [shard]
        for _ in range(1, grid.depth):
            column.append(grid.along_z(column[-1], 1))
        columns.append(column)
    return jnp.stack([jnp.concatenate(parts, axis=1) for parts in zip(*columns)])


def gather_near(grid, column):
    return grid.over_x(column), grid.over_y(column)


def gather_far(grid, by_x, by_y):
    half = grid.depth // 2
    return grid.over_y(by_x[:half]), grid.over_x(by_y[half:])


def swap(grid, *parts):
    return [grid.over_core(part) for part in parts]


def assemble(grid, widths, column, near, far, swapped):
    parts = []
    half = grid.depth // 2
    for part, other, first, flip_x, flip_y in zip(
        (column, *near, *far),
        (*swapped, *swap(grid, *far)),
        (0, 0, 0, 0, half),
        (0, 1, 0, 1, 1),
        (0, 0, 1, 1, 1),
    ):
        parts.append((part, first, flip_x, flip_y, 0))
        parts.append((other, first, flip_x, flip_y, 1))
    places = [where[1:] for where in parts]
    parts = [part for part, *_ in parts]
    depth, rows, _ = column.shape
    if rows % 16 == 0:
        wholes = assemble_by_copies(depth, places, widths, parts)
    else:
        whole = jnp.zeros((depth, 2, 2, 2) + column.shape[1:], column.dtype)
        for part, (first, flip_x, flip_y, flip_core) in zip(parts, places):
            for k in range(part.shape[0]):
                where = ((grid.z - first - k) % depth, grid.y ^ flip_y, grid.x ^ flip_x, grid.core ^ flip_core)
                whole = lax.dynamic_update_slice(whole, part[k][None, None, None, None], where + (0, 0))
        starts = [sum(widths[:i]) for i in range(len(widths))]
        wholes = [whole[..., start : start + width] for start, width in zip(starts, widths)]
    return [whole.reshape(-1, width) for whole, width in zip(wholes, widths)]


def assemble_by_copies(depth, places, widths, parts):
    rows, wide = parts[0].shape[1:]
    blocks = sum(part.shape[0] for part in parts)
    starts = [sum(widths[:i]) for i in range(len(widths))]

    def kernel(*refs):
        sources, targets = refs[: len(parts)], refs[len(parts) : -3]
        held, came, went = refs[-3:]
        place, spot = lax.axis_index("dp"), lax.axis_index("seq")
        z, y, x, core = place // 2, place % 2, spot // 2, spot % 2
        steps = []
        for source, (first, flip_x, flip_y, flip_core) in zip(sources, places):
            across_y = 1 - y if flip_y else y
            across_x = 1 - x if flip_x else x
            across_core = 1 - core if flip_core else core
            for k in range(source.shape[0]):
                height = lax.rem(z + (2 * depth - first - k), depth)
                slot = len(steps)
                read = pltpu.make_async_copy(source.at[k], held.at[slot], came.at[slot])
                read.start()
                steps.append((read, (height, across_y, across_x, across_core)))
        writes = []
        for slot, (read, where) in enumerate(steps):
            read.wait()
            for i, target in enumerate(targets):
                write = pltpu.make_async_copy(
                    held.at[slot, :, starts[i] : starts[i] + widths[i]],
                    target.at[where],
                    went.at[slot, i],
                )
                write.start()
                writes.append(write)
        for write in writes:
            write.wait()

    shapes = [jax.ShapeDtypeStruct((depth, 2, 2, 2, rows, width), parts[0].dtype) for width in widths]
    return pl.pallas_call(
        kernel,
        in_specs=[pl.BlockSpec(memory_space=pl.ANY)] * len(parts),
        out_specs=[pl.BlockSpec(memory_space=pl.ANY)] * len(widths),
        out_shape=shapes,
        scratch_shapes=[
            pltpu.VMEM((blocks, rows, wide), parts[0].dtype),
            pltpu.SemaphoreType.DMA((blocks,)),
            pltpu.SemaphoreType.DMA((blocks, len(widths))),
        ],
        compiler_params=pltpu.CompilerParams(vmem_limit_bytes=32 * 2**20),
        cost_estimate=pl.CostEstimate(
            flops=0, bytes_accessed=4 * sum(part.size for part in parts), transcendentals=0
        ),
        name="assemble",
    )(*parts)


def reduce_core(grid, terms):
    terms = terms.reshape(grid.depth, 2, 2, 2, -1, terms.shape[-1])
    return add(pick(terms, grid.core, 3), grid.over_core(pick(terms, 1 - grid.core, 3)))


def block_at(total, y, x):
    return pick(pick(total, y, 1), x, 1)


def reduce_far(grid, total, by_x):
    part = grid.depth * by_x // 4
    far = block_at(total, 1 - grid.y, 1 - grid.x)
    return (grid.over_x(far[:part]) if part else None), grid.over_y(far[part:])


def reduce_near(grid, total, far):
    from_x, from_y = far
    to_x = block_at(total, grid.y, 1 - grid.x)
    to_y = block_at(total, 1 - grid.y, grid.x)
    part = 0 if from_x is None else from_x.shape[0]
    to_x = jnp.concatenate([to_x[:part], add(to_x[part:], from_y)])
    if part:
        to_y = jnp.concatenate([add(to_y[:part], from_x), to_y[part:]])
    return grid.over_x(to_x), grid.over_y(to_y)


def reduce_z(grid, total, near):
    own = block_at(total, grid.y, grid.x).astype(F32) + near[0].astype(F32) + near[1].astype(F32)
    low = own.astype(total.dtype)
    result = pick(own, grid.z, 0)
    for step in range(1, grid.depth):
        sent = pick(low, (grid.z + step) % grid.depth, 0)
        result = result + grid.along_z(sent, step).astype(F32)
    return result


def reduce_small(grid, terms):
    total = terms.reshape((grid.depth, 2, 2, 2) + terms.shape[1:])
    total = pick(total, grid.core, 3) + grid.over_core(pick(total, 1 - grid.core, 3))
    total = pick(total, grid.x, 2) + grid.over_x(pick(total, 1 - grid.x, 2))
    total = pick(total, grid.y, 1) + grid.over_y(pick(total, 1 - grid.y, 1))
    result = pick(total, grid.z, 0)
    for step in range(1, grid.depth):
        result = result + grid.along_z(pick(total, (grid.z + step) % grid.depth, 0), step)
    return result


def dot_rows(left, right):
    return lax.dot_general(left, right, (((1,), (1,)), ((), ())), preferred_element_type=F32)


def dot_columns(left, right):
    return lax.dot_general(left, right, (((0,), (0,)), ((), ())), preferred_element_type=F32)


def attend_forward_kernel(keep_ref, q_ref, k_ref, v_ref, out_ref, log_ref):
    keep = keep_ref[0] > 0
    queries = q_ref[0, 0]
    keys = k_ref[:, 0].reshape(-1, PAIR)
    values = v_ref[:, 0].reshape(-1, PAIR)
    outs, logs = [], []
    for head in range(2):
        part = slice(head * HEAD_DIM, (head + 1) * HEAD_DIM)
        scores = dot_rows(queries[:, part] * SCALE, keys[:, part])
        scores = jnp.where(keep, scores, MASKED)
        largest = jnp.max(scores, axis=-1, keepdims=True)
        raised = jnp.exp(scores - largest)
        totals = jnp.sum(raised, axis=-1, keepdims=True)
        mixed = jnp.dot(raised.astype(BF16), values[:, part], preferred_element_type=F32)
        outs.append(mixed / totals)
        logs.append(largest + jnp.log(totals))
    out_ref[0] = jnp.concatenate(outs, axis=1).astype(BF16)
    log_ref[0, 0] = jnp.concatenate(logs, axis=1)


def attend_forward(slot, projected, keep):
    blocks, _, local_len, wide = projected.shape
    width = wide // 3
    pairs = width // PAIR
    full_len = blocks * local_len
    return pl.pallas_call(
        attend_forward_kernel,
        grid=(pairs,),
        in_specs=[
            pl.BlockSpec((1, 1, full_len), lambda p: (slot, 0, 0)),
            pl.BlockSpec((1, 1, local_len, PAIR), lambda p: (0, slot, 0, p)),
            pl.BlockSpec((blocks, 1, local_len, PAIR), lambda p: (0, slot, 0, pairs + p)),
            pl.BlockSpec((blocks, 1, local_len, PAIR), lambda p: (0, slot, 0, 2 * pairs + p)),
        ],
        out_specs=[
            pl.BlockSpec((1, local_len, PAIR), lambda p: (0, 0, p)),
            pl.BlockSpec((1, 1, local_len, 2), lambda p: (0, p, 0, 0)),
        ],
        out_shape=[
            jax.ShapeDtypeStruct((1, local_len, width), BF16),
            jax.ShapeDtypeStruct((1, pairs, local_len, 2), F32),
        ],
        cost_estimate=QUICK,
        compiler_params=pltpu.CompilerParams(vmem_limit_bytes=32 * 2**20),
        name="attend_forward",
    )(keep, projected, projected, projected)


def attend_backward_kernel(keep_ref, q_ref, k_ref, v_ref, log_ref, g_ref, dq_ref, own_ref, send_ref):
    keep = keep_ref[0] > 0
    blocks, _, local_len, _ = k_ref.shape
    queries = q_ref[0, 0]
    keys = k_ref[:, 0].reshape(-1, PAIR)
    values = v_ref[:, 0].reshape(-1, PAIR)
    grads = g_ref[0]
    logs = log_ref[0, 0]
    dqs, dks, dvs = [], [], []
    for head in range(2):
        part = slice(head * HEAD_DIM, (head + 1) * HEAD_DIM)
        scaled = queries[:, part] * SCALE
        scores = jnp.where(keep, dot_rows(scaled, keys[:, part]), MASKED)
        chance = jnp.exp(scores - logs[:, head : head + 1])
        grad_chance = dot_rows(grads[:, part], values[:, part])
        product = chance * grad_chance
        inner = jnp.sum(product, axis=-1, keepdims=True)
        grad_scores = jnp.where(keep, product - chance * inner, 0.0).astype(BF16)
        dqs.append(jnp.dot(grad_scores, keys[:, part], preferred_element_type=F32) * SCALE)
        dks.append(dot_columns(scaled, grad_scores))
        dvs.append(dot_columns(grads[:, part], chance.astype(BF16)))
    dq_ref[0] = jnp.concatenate(dqs, axis=1).astype(BF16)
    for kind, terms in enumerate((dks, dvs)):
        turned = jnp.concatenate(terms, axis=0).T.astype(BF16).reshape(blocks, local_len, PAIR)
        for block in range(blocks):
            target = send_ref if block % 2 else own_ref
            target[block // 2, kind] = turned[block]


def attend_backward(slot, projected, keep, logs, grad_attended):
    blocks, slots, local_len, wide = projected.shape
    width = wide // 3
    pairs = width // PAIR
    full_len = blocks * local_len
    terms = jax.ShapeDtypeStruct((blocks // 2, 2, local_len, width), BF16)
    terms_spec = pl.BlockSpec((blocks // 2, 2, local_len, PAIR), lambda p: (0, 0, 0, p))
    return pl.pallas_call(
        attend_backward_kernel,
        grid=(pairs,),
        in_specs=[
            pl.BlockSpec((1, 1, full_len), lambda p: (slot, 0, 0)),
            pl.BlockSpec((1, 1, local_len, PAIR), lambda p: (0, slot, 0, p)),
            pl.BlockSpec((blocks, 1, local_len, PAIR), lambda p: (0, slot, 0, pairs + p)),
            pl.BlockSpec((blocks, 1, local_len, PAIR), lambda p: (0, slot, 0, 2 * pairs + p)),
            pl.BlockSpec((1, 1, local_len, 2), lambda p: (0, p, 0, 0)),
            pl.BlockSpec((1, local_len, PAIR), lambda p: (slot, 0, p)),
        ],
        out_specs=[pl.BlockSpec((1, local_len, PAIR), lambda p: (0, 0, p)), terms_spec, terms_spec],
        out_shape=[jax.ShapeDtypeStruct((1, local_len, width), BF16), terms, terms],
        cost_estimate=QUICK,
        compiler_params=pltpu.CompilerParams(vmem_limit_bytes=32 * 2**20),
        name="attend_backward",
    )(keep, projected, projected, projected, logs, grad_attended)


def normalise(values):
    average = jnp.mean(values, axis=-1, keepdims=True)
    centred = values - average
    spread = jnp.mean(centred * centred, axis=-1, keepdims=True)
    scale = lax.rsqrt(spread + EPS)
    return centred * scale, scale


def normalise_back(grad, gain, normal, scale):
    inward = grad * gain
    mean_in = jnp.mean(inward, axis=-1, keepdims=True)
    mean_normal = jnp.mean(inward * normal, axis=-1, keepdims=True)
    values = scale * (inward - mean_in - normal * mean_normal)
    return values, jnp.sum(grad * normal, axis=0), jnp.sum(grad, axis=0)


def split_vectors(table, lengths):
    pieces, offset = [], 0
    for length in lengths:
        pieces.append(table[:, offset : offset + length].reshape(-1))
        offset += length
    return pieces


LANES = 128


def fold(vectors, rows):
    groups, count = vectors.shape
    per_row = -(-count // rows)
    vectors = jnp.pad(vectors, ((0, 0), (0, per_row * rows - count)))
    return jnp.pad(vectors.reshape(groups * rows, per_row), ((0, 0), (0, LANES - per_row)))


def unfold(block, rows, count):
    per_row = -(-count // rows)
    return block[:, :per_row].reshape(-1, per_row * rows)[:, :count]


def shards(
    tokens,
    cotangent,
    token_mask,
    w_qkv,
    w_out,
    w_fc1,
    w_fc2,
    b_q,
    b_v,
    b_out,
    b_fc1,
    b_fc2,
    ln1_gain,
    ln1_shift,
    ln2_gain,
    ln2_shift,
):
    grid = Grid()
    groups = grid.dp * grid.seq
    slots, local_len, width = tokens.shape
    count = slots * local_len
    vector_shards = (b_q, b_v, b_out, b_fc1, b_fc2, ln1_gain, ln1_shift, ln2_gain, ln2_shift)
    lengths = [vector.shape[0] for vector in vector_shards]

    total_len = sum(lengths)
    depth_rows = w_qkv.shape[0]

    vectors = fold(jnp.concatenate(vector_shards)[None], depth_rows)
    column_one = gather_z(grid, w_qkv, vectors)
    by_core, by_x = grid.over_core(tokens), grid.over_x(tokens)
    column_one, by_x = lax.optimization_barrier((column_one, by_x))
    near_one = gather_near(grid, column_one)
    column_two = gather_z(grid, after(jnp.concatenate([w_out, w_fc1], axis=1), column_one, by_x))
    near_one = lax.optimization_barrier(near_one)
    far_one = gather_far(grid, *near_one)
    seen = jnp.stack([tokens, by_core, by_x, grid.over_core(by_x)])
    full_qkv, vectors = assemble(
        grid, (w_qkv.shape[1], LANES), column_one, near_one, far_one, swap(grid, column_one, *near_one)
    )
    column_two = after(column_two, far_one)
    near_two = gather_near(grid, column_two)
    column_three = gather_z(grid, after(w_fc2, column_two))
    near_two = lax.optimization_barrier(near_two)
    far_two = gather_far(grid, *near_two)

    vectors = unfold(vectors, depth_rows, total_len)
    vectors = [v.astype(F32) for v in split_vectors(vectors, lengths)]
    bias_q, bias_v, bias_out, bias_fc1, bias_fc2, gain_one, shift_one, gain_two, shift_two = vectors
    spot = lax.axis_index("seq")
    blocks = grid.seq
    mask_blocks = token_mask.reshape(slots, blocks, local_len)
    keep = jnp.stack([pick(mask_blocks, spot ^ block, 1) for block in range(blocks)], 1)
    valid = (keep[:, 0] > 0).reshape(-1, 1).astype(F32)
    keep = keep.reshape(slots, 1, -1)

    rows = tokens.reshape(-1, width).astype(F32)
    normal_seen, _ = normalise(seen.reshape(-1, width).astype(F32))
    normed_seen = lax.optimization_barrier((normal_seen * gain_one + shift_one).astype(BF16))
    normed_low = normed_seen[:count]
    qkv_bias = jnp.concatenate([bias_q, jnp.zeros_like(bias_out), bias_v])
    projected = (jnp.dot(normed_seen, full_qkv, preferred_element_type=F32) + qkv_bias).astype(BF16)
    projected = projected.reshape(blocks, slots, local_len, 3 * width)

    swapped_two = swap(grid, column_two, *near_two)
    projected, column_three, far_two, swapped_two = lax.optimization_barrier(
        (projected, column_three, far_two, swapped_two)
    )
    near_three = gather_near(grid, column_three)
    full_out, full_fc1 = assemble(
        grid, (width, w_fc1.shape[1]), column_two, near_two, far_two, swapped_two
    )
    attended, logs = zip(*[attend_forward(slot, projected, keep) for slot in range(slots)])
    attended = jnp.concatenate(attended).reshape(-1, width)
    attended, near_three = lax.optimization_barrier((attended, near_three))
    far_three = gather_far(grid, *near_three)
    swapped_three = swap(grid, column_three, *near_three)
    middle = rows + jnp.dot(attended, full_out, preferred_element_type=F32) + bias_out
    normal_two, scale_two = normalise(middle)
    second_low = (normal_two * gain_two + shift_two).astype(BF16)
    hidden = jnp.dot(second_low, full_fc1, preferred_element_type=F32) + bias_fc1
    below = 0.5 * (1.0 + lax.erf(hidden * math.sqrt(0.5)))
    density = jnp.exp(-0.5 * hidden * hidden) * (1.0 / math.sqrt(2.0 * math.pi))
    activated_low = (hidden * below).astype(BF16)
    slope = (below + hidden * density).astype(BF16)
    activated_low, slope, far_three, swapped_three = lax.optimization_barrier(
        (activated_low, slope, far_three, swapped_three)
    )
    (full_fc2,) = assemble(grid, (width,), column_three, near_three, far_three, swapped_three)

    grad_y_low = cotangent.reshape(-1, width) * valid.astype(BF16)
    grad_y = grad_y_low.astype(F32)
    terms_fc2 = dot_columns(activated_low, grad_y_low).astype(BF16)
    sum_fc2 = reduce_core(grid, terms_fc2)
    grad_y_next, full_fc2 = after((grad_y_low, full_fc2), terms_fc2)
    grad_hidden = (dot_rows(grad_y_next, full_fc2) * slope.astype(F32)).astype(BF16)
    grad_hidden, sum_fc2 = lax.optimization_barrier((grad_hidden, sum_fc2))
    far_fc2 = reduce_far(grid, sum_fc2, 2)
    grad_b_fc2 = jnp.sum(grad_y, axis=0)
    terms_fc1 = dot_columns(second_low, grad_hidden).astype(BF16)
    grad_b_fc1 = jnp.sum(grad_hidden.astype(F32), axis=0)
    grad_second = dot_rows(after(grad_hidden, terms_fc1), full_fc1)
    grad_middle, grad_gain_two, grad_shift_two = normalise_back(
        grad_second, gain_two, normal_two, scale_two
    )
    grad_middle = grad_y + grad_middle
    grad_branch = after(grad_middle.astype(BF16), far_fc2)
    near_fc2 = reduce_near(grid, sum_fc2, far_fc2)
    grad_b_out = jnp.sum(grad_branch.astype(F32), axis=0)
    terms_out = dot_columns(attended, grad_branch).astype(BF16)
    sum_two = jnp.concatenate([reduce_core(grid, terms_out), reduce_core(grid, terms_fc1)], axis=-1)
    grad_attended = dot_rows(grad_branch, full_out).astype(BF16).reshape(slots, local_len, width)

    parts, ahead = [], sum_two
    for slot in range(slots):
        grad_attended = after(grad_attended, ahead)
        grad_queries, own, send = attend_backward(slot, projected, keep, logs[slot], grad_attended)
        if slot:
            send = after(send, parts[-1][3])
        came = grid.over_core(send)
        across = add(own[1], came[1])
        ahead = (grad_queries, across) if slot == 0 else (grad_queries, across, parts[-1][3])
        if slot == 0:
            near_fc2 = after(near_fc2, grad_queries)
            far_two = reduce_far(grid, after(sum_two, near_fc2), 0)
            grad_w_fc2 = reduce_z(grid, sum_fc2, near_fc2)
            ahead = (grad_queries,)
        else:
            ahead = (grad_queries, parts[-1][4])
        parts.append((grad_queries, own[0], came[0], grid.over_x(across), across))
    activated_late = after(activated_low, parts[-1][4])
    result = (
        middle + jnp.dot(activated_late, full_fc2, preferred_element_type=F32) + bias_fc2
    ) * valid
    out_tokens = result.astype(BF16).reshape(slots, local_len, width)
    near_two = reduce_near(grid, sum_two, far_two)
    grad_two = reduce_z(grid, sum_two, near_two)
    grad_w_out, grad_w_fc1 = grad_two[:, :width], grad_two[:, width:]

    grad_queries = jnp.concatenate([part[0] for part in parts]).reshape(-1, width)
    terms_q = dot_columns(normed_low, grad_queries).astype(BF16)
    sum_q = reduce_core(grid, terms_q)
    far_q = reduce_far(grid, sum_q, 0)
    grad_keys_values = [
        (own.astype(F32) + came.astype(F32) + across.astype(F32)).astype(BF16)
        for _, own, came, across, _ in parts
    ]
    grad_keys, grad_values = [jnp.stack([part[kind] for part in grad_keys_values]) for kind in range(2)]
    grad_kv = jnp.concatenate([grad_keys, grad_values], axis=-1).reshape(-1, 2 * width)
    grad_kv, grad_w_fc2 = lax.optimization_barrier((grad_kv, grad_w_fc2))
    terms_kv = dot_columns(normed_low, grad_kv).astype(BF16)
    sum_kv = reduce_core(grid, terms_kv)
    far_kv = reduce_far(grid, sum_kv, 2)
    grad_qkv = after(jnp.concatenate([grad_queries, grad_kv], axis=-1), terms_kv)
    grad_normed = dot_rows(grad_qkv, full_qkv)
    grad_qkv_wide = jnp.sum(grad_qkv.astype(F32), axis=0)
    grad_b_q = grad_qkv_wide[:width]
    grad_b_v = grad_qkv_wide[2 * width :]
    normal_one, scale_one = normalise(rows)
    grad_rows, grad_gain_one, grad_shift_one = normalise_back(
        grad_normed, gain_one, normal_one, scale_one
    )
    grad_tokens = (grad_middle + grad_rows).reshape(slots, local_len, width)
    terms = (
        grad_b_q,
        grad_b_v,
        grad_b_out,
        grad_b_fc1,
        grad_b_fc2,
        grad_gain_one,
        grad_shift_one,
        grad_gain_two,
        grad_shift_two,
    )
    terms = jnp.concatenate([term.reshape(groups, -1) for term in terms], axis=-1)
    owned = split_vectors(reduce_small(grid, terms[:, None]).reshape(1, -1), lengths)
    near_q = reduce_near(grid, sum_q, far_q)
    near_kv = reduce_near(grid, sum_kv, far_kv)
    grad_w_qkv = jnp.concatenate([reduce_z(grid, sum_q, near_q), reduce_z(grid, sum_kv, near_kv)], axis=-1)
    return (out_tokens, grad_tokens, grad_w_qkv, grad_w_out, grad_w_fc1, grad_w_fc2, *owned)


def solution(mesh):
    spread = P(("dp", "seq"))
    row = P("dp", "seq", None)
    matrix = P(("dp", "seq"), None)
    in_specs = (row, row, P("dp", None)) + (matrix,) * 4 + (spread,) * 9
    out_specs = (row, row) + (matrix,) * 4 + (spread,) * 9
    return jax.shard_map(shards, mesh=mesh, in_specs=in_specs, out_specs=out_specs, check_vma=False)
```

```python
import math

import jax
import jax.numpy as jnp
from jax import lax
from jax.experimental import pallas as pl
from jax.experimental.pallas import tpu as pltpu
from jax.sharding import PartitionSpec as P

HEAD_DIM = 64
PAIR = 2 * HEAD_DIM
EPS = 1e-06
MASKED = -1000000000.0
SCALE = 1.0 / math.sqrt(HEAD_DIM)
F32 = jnp.float32
BF16 = jnp.bfloat16
QUICK = pl.CostEstimate(flops=0, bytes_accessed=0, transcendentals=0)


def after(values, *others):
    return lax.optimization_barrier((values, others))[0]


class Grid:
    def __init__(self):
        self.dp, self.seq = lax.axis_size("dp"), lax.axis_size("seq")
        self.depth = self.dp // 2
        place, spot = lax.axis_index("dp"), lax.axis_index("seq")
        self.z, self.y = place // 2, place % 2
        self.x, self.core = spot // 2, spot % 2

    def over_core(self, values):
        return lax.ppermute(values, "seq", [(i, i ^ 1) for i in range(self.seq)])

    def over_x(self, values):
        return lax.ppermute(values, "seq", [(i, i ^ 2) for i in range(self.seq)])

    def over_y(self, values):
        return lax.ppermute(values, "dp", [(i, i ^ 1) for i in range(self.dp)])

    def along_z(self, values, step):
        return lax.ppermute(values, "dp", [(i, (i + 2 * step) % self.dp) for i in range(self.dp)])


def pick(values, index, axis):
    return lax.dynamic_index_in_dim(values, index, axis, keepdims=False)


def add(left, right):
    return (left.astype(F32) + right.astype(F32)).astype(left.dtype)


def gather_z(grid, *shards):
    columns = []
    for shard in shards:
        column = [shard]
        for _ in range(1, grid.depth):
            column.append(grid.along_z(column[-1], 1))
        columns.append(column)
    return jnp.stack([jnp.concatenate(parts, axis=1) for parts in zip(*columns)])


def gather_near(grid, column):
    return grid.over_x(column), grid.over_y(column)


def gather_far(grid, by_x, by_y):
    half = grid.depth // 2
    return grid.over_y(by_x[:half]), grid.over_x(by_y[half:])


def assemble(grid, widths, column, near, far):
    parts = []
    half = grid.depth // 2
    for part, first, flip_x, flip_y in (
        (column, 0, 0, 0),
        (near[0], 0, 1, 0),
        (near[1], 0, 0, 1),
        (far[0], 0, 1, 1),
        (far[1], half, 1, 1),
    ):
        parts.append((part, first, flip_x, flip_y, 0))
        parts.append((grid.over_core(part), first, flip_x, flip_y, 1))
    places = [where[1:] for where in parts]
    parts = [part for part, *_ in parts]
    depth, rows, _ = column.shape
    if rows % 16 == 0:
        wholes = assemble_by_copies(depth, places, widths, parts)
    else:
        whole = jnp.zeros((depth, 2, 2, 2) + column.shape[1:], column.dtype)
        for part, (first, flip_x, flip_y, flip_core) in zip(parts, places):
            for k in range(part.shape[0]):
                where = ((grid.z - first - k) % depth, grid.y ^ flip_y, grid.x ^ flip_x, grid.core ^ flip_core)
                whole = lax.dynamic_update_slice(whole, part[k][None, None, None, None], where + (0, 0))
        starts = [sum(widths[:i]) for i in range(len(widths))]
        wholes = [whole[..., start : start + width] for start, width in zip(starts, widths)]
    return [whole.reshape(-1, width) for whole, width in zip(wholes, widths)]


def assemble_by_copies(depth, places, widths, parts):
    rows, wide = parts[0].shape[1:]
    blocks = sum(part.shape[0] for part in parts)
    starts = [sum(widths[:i]) for i in range(len(widths))]

    def kernel(*refs):
        sources, targets = refs[: len(parts)], refs[len(parts) : -3]
        held, came, went = refs[-3:]
        place, spot = lax.axis_index("dp"), lax.axis_index("seq")
        z, y, x, core = place // 2, place % 2, spot // 2, spot % 2
        steps = []
        for source, (first, flip_x, flip_y, flip_core) in zip(sources, places):
            across_y = 1 - y if flip_y else y
            across_x = 1 - x if flip_x else x
            across_core = 1 - core if flip_core else core
            for k in range(source.shape[0]):
                height = lax.rem(z + (2 * depth - first - k), depth)
                slot = len(steps)
                read = pltpu.make_async_copy(source.at[k], held.at[slot], came.at[slot])
                read.start()
                steps.append((read, (height, across_y, across_x, across_core)))
        writes = []
        for slot, (read, where) in enumerate(steps):
            read.wait()
            for i, target in enumerate(targets):
                write = pltpu.make_async_copy(
                    held.at[slot, :, starts[i] : starts[i] + widths[i]],
                    target.at[where],
                    went.at[slot, i],
                )
                write.start()
                writes.append(write)
        for write in writes:
            write.wait()

    shapes = [jax.ShapeDtypeStruct((depth, 2, 2, 2, rows, width), parts[0].dtype) for width in widths]
    return pl.pallas_call(
        kernel,
        in_specs=[pl.BlockSpec(memory_space=pl.ANY)] * len(parts),
        out_specs=[pl.BlockSpec(memory_space=pl.ANY)] * len(widths),
        out_shape=shapes,
        scratch_shapes=[
            pltpu.VMEM((blocks, rows, wide), parts[0].dtype),
            pltpu.SemaphoreType.DMA((blocks,)),
            pltpu.SemaphoreType.DMA((blocks, len(widths))),
        ],
        compiler_params=pltpu.CompilerParams(vmem_limit_bytes=32 * 2**20),
        cost_estimate=pl.CostEstimate(
            flops=0, bytes_accessed=4 * sum(part.size for part in parts), transcendentals=0
        ),
        name="assemble",
    )(*parts)


def reduce_core(grid, terms):
    terms = terms.reshape(grid.depth, 2, 2, 2, -1, terms.shape[-1])
    return add(pick(terms, grid.core, 3), grid.over_core(pick(terms, 1 - grid.core, 3)))


def block_at(total, y, x):
    return pick(pick(total, y, 1), x, 1)


def reduce_far(grid, total, by_x):
    part = grid.depth * by_x // 4
    far = block_at(total, 1 - grid.y, 1 - grid.x)
    return (grid.over_x(far[:part]) if part else None), grid.over_y(far[part:])


def reduce_near(grid, total, far):
    from_x, from_y = far
    to_x = block_at(total, grid.y, 1 - grid.x)
    to_y = block_at(total, 1 - grid.y, grid.x)
    part = 0 if from_x is None else from_x.shape[0]
    to_x = jnp.concatenate([to_x[:part], add(to_x[part:], from_y)])
    if part:
        to_y = jnp.concatenate([add(to_y[:part], from_x), to_y[part:]])
    return grid.over_x(to_x), grid.over_y(to_y)


def reduce_z(grid, total, near):
    own = block_at(total, grid.y, grid.x).astype(F32) + near[0].astype(F32) + near[1].astype(F32)
    low = own.astype(total.dtype)
    result = pick(own, grid.z, 0)
    for step in range(1, grid.depth):
        sent = pick(low, (grid.z + step) % grid.depth, 0)
        result = result + grid.along_z(sent, step).astype(F32)
    return result


def reduce_small(grid, terms):
    total = terms.reshape((grid.depth, 2, 2, 2) + terms.shape[1:])
    total = pick(total, grid.core, 3) + grid.over_core(pick(total, 1 - grid.core, 3))
    total = pick(total, grid.x, 2) + grid.over_x(pick(total, 1 - grid.x, 2))
    total = pick(total, grid.y, 1) + grid.over_y(pick(total, 1 - grid.y, 1))
    result = pick(total, grid.z, 0)
    for step in range(1, grid.depth):
        result = result + grid.along_z(pick(total, (grid.z + step) % grid.depth, 0), step)
    return result


def dot_rows(left, right):
    return lax.dot_general(left, right, (((1,), (1,)), ((), ())), preferred_element_type=F32)


def dot_columns(left, right):
    return lax.dot_general(left, right, (((0,), (0,)), ((), ())), preferred_element_type=F32)


def attend_forward_kernel(keep_ref, q_ref, k_ref, v_ref, out_ref, log_ref):
    keep = keep_ref[0] > 0
    queries = q_ref[0, 0]
    keys = k_ref[:, 0].reshape(-1, PAIR)
    values = v_ref[:, 0].reshape(-1, PAIR)
    outs, logs = [], []
    for head in range(2):
        part = slice(head * HEAD_DIM, (head + 1) * HEAD_DIM)
        scores = dot_rows(queries[:, part] * SCALE, keys[:, part])
        scores = jnp.where(keep, scores, MASKED)
        largest = jnp.max(scores, axis=-1, keepdims=True)
        raised = jnp.exp(scores - largest)
        totals = jnp.sum(raised, axis=-1, keepdims=True)
        mixed = jnp.dot(raised.astype(BF16), values[:, part], preferred_element_type=F32)
        outs.append(mixed / totals)
        logs.append(largest + jnp.log(totals))
    out_ref[0] = jnp.concatenate(outs, axis=1).astype(BF16)
    log_ref[0, 0] = jnp.concatenate(logs, axis=1)


def attend_forward(slot, projected, keep):
    blocks, _, local_len, wide = projected.shape
    width = wide // 3
    pairs = width // PAIR
    full_len = blocks * local_len
    return pl.pallas_call(
        attend_forward_kernel,
        grid=(pairs,),
        in_specs=[
            pl.BlockSpec((1, 1, full_len), lambda p: (slot, 0, 0)),
            pl.BlockSpec((1, 1, local_len, PAIR), lambda p: (0, slot, 0, p)),
            pl.BlockSpec((blocks, 1, local_len, PAIR), lambda p: (0, slot, 0, pairs + p)),
            pl.BlockSpec((blocks, 1, local_len, PAIR), lambda p: (0, slot, 0, 2 * pairs + p)),
        ],
        out_specs=[
            pl.BlockSpec((1, local_len, PAIR), lambda p: (0, 0, p)),
            pl.BlockSpec((1, 1, local_len, 2), lambda p: (0, p, 0, 0)),
        ],
        out_shape=[
            jax.ShapeDtypeStruct((1, local_len, width), BF16),
            jax.ShapeDtypeStruct((1, pairs, local_len, 2), F32),
        ],
        cost_estimate=QUICK,
        compiler_params=pltpu.CompilerParams(vmem_limit_bytes=32 * 2**20),
        name="attend_forward",
    )(keep, projected, projected, projected)


def attend_backward_kernel(keep_ref, q_ref, k_ref, v_ref, log_ref, g_ref, dq_ref, own_ref, send_ref):
    keep = keep_ref[0] > 0
    blocks, _, local_len, _ = k_ref.shape
    queries = q_ref[0, 0]
    keys = k_ref[:, 0].reshape(-1, PAIR)
    values = v_ref[:, 0].reshape(-1, PAIR)
    grads = g_ref[0]
    logs = log_ref[0, 0]
    dqs, dks, dvs = [], [], []
    for head in range(2):
        part = slice(head * HEAD_DIM, (head + 1) * HEAD_DIM)
        scaled = queries[:, part] * SCALE
        scores = jnp.where(keep, dot_rows(scaled, keys[:, part]), MASKED)
        chance = jnp.exp(scores - logs[:, head : head + 1])
        grad_chance = dot_rows(grads[:, part], values[:, part])
        product = chance * grad_chance
        inner = jnp.sum(product, axis=-1, keepdims=True)
        grad_scores = jnp.where(keep, product - chance * inner, 0.0).astype(BF16)
        dqs.append(jnp.dot(grad_scores, keys[:, part], preferred_element_type=F32) * SCALE)
        dks.append(dot_columns(scaled, grad_scores))
        dvs.append(dot_columns(grads[:, part], chance.astype(BF16)))
    dq_ref[0] = jnp.concatenate(dqs, axis=1).astype(BF16)
    for kind, terms in enumerate((dks, dvs)):
        turned = jnp.concatenate(terms, axis=0).T.astype(BF16).reshape(blocks, local_len, PAIR)
        for block in range(blocks):
            target = send_ref if block % 2 else own_ref
            target[block // 2, kind] = turned[block]


def attend_backward(slot, projected, keep, logs, grad_attended):
    blocks, slots, local_len, wide = projected.shape
    width = wide // 3
    pairs = width // PAIR
    full_len = blocks * local_len
    terms = jax.ShapeDtypeStruct((blocks // 2, 2, local_len, width), BF16)
    terms_spec = pl.BlockSpec((blocks // 2, 2, local_len, PAIR), lambda p: (0, 0, 0, p))
    return pl.pallas_call(
        attend_backward_kernel,
        grid=(pairs,),
        in_specs=[
            pl.BlockSpec((1, 1, full_len), lambda p: (slot, 0, 0)),
            pl.BlockSpec((1, 1, local_len, PAIR), lambda p: (0, slot, 0, p)),
            pl.BlockSpec((blocks, 1, local_len, PAIR), lambda p: (0, slot, 0, pairs + p)),
            pl.BlockSpec((blocks, 1, local_len, PAIR), lambda p: (0, slot, 0, 2 * pairs + p)),
            pl.BlockSpec((1, 1, local_len, 2), lambda p: (0, p, 0, 0)),
            pl.BlockSpec((1, local_len, PAIR), lambda p: (slot, 0, p)),
        ],
        out_specs=[pl.BlockSpec((1, local_len, PAIR), lambda p: (0, 0, p)), terms_spec, terms_spec],
        out_shape=[jax.ShapeDtypeStruct((1, local_len, width), BF16), terms, terms],
        cost_estimate=QUICK,
        compiler_params=pltpu.CompilerParams(vmem_limit_bytes=32 * 2**20),
        name="attend_backward",
    )(keep, projected, projected, projected, logs, grad_attended)


def normalise(values):
    average = jnp.mean(values, axis=-1, keepdims=True)
    centred = values - average
    spread = jnp.mean(centred * centred, axis=-1, keepdims=True)
    scale = lax.rsqrt(spread + EPS)
    return centred * scale, scale


def normalise_back(grad, gain, normal, scale):
    inward = grad * gain
    mean_in = jnp.mean(inward, axis=-1, keepdims=True)
    mean_normal = jnp.mean(inward * normal, axis=-1, keepdims=True)
    values = scale * (inward - mean_in - normal * mean_normal)
    return values, jnp.sum(grad * normal, axis=0), jnp.sum(grad, axis=0)


def split_vectors(table, lengths):
    pieces, offset = [], 0
    for length in lengths:
        pieces.append(table[:, offset : offset + length].reshape(-1))
        offset += length
    return pieces


LANES = 128


def fold(vectors, rows):
    groups, count = vectors.shape
    per_row = -(-count // rows)
    vectors = jnp.pad(vectors, ((0, 0), (0, per_row * rows - count)))
    return jnp.pad(vectors.reshape(groups * rows, per_row), ((0, 0), (0, LANES - per_row)))


def unfold(block, rows, count):
    per_row = -(-count // rows)
    return block[:, :per_row].reshape(-1, per_row * rows)[:, :count]


def shards(
    tokens,
    cotangent,
    token_mask,
    w_qkv,
    w_out,
    w_fc1,
    w_fc2,
    b_q,
    b_v,
    b_out,
    b_fc1,
    b_fc2,
    ln1_gain,
    ln1_shift,
    ln2_gain,
    ln2_shift,
):
    grid = Grid()
    groups = grid.dp * grid.seq
    slots, local_len, width = tokens.shape
    count = slots * local_len
    vector_shards = (b_q, b_v, b_out, b_fc1, b_fc2, ln1_gain, ln1_shift, ln2_gain, ln2_shift)
    lengths = [vector.shape[0] for vector in vector_shards]

    total_len = sum(lengths)
    depth_rows = w_qkv.shape[0]

    vectors = fold(jnp.concatenate(vector_shards)[None], depth_rows)
    column_one = gather_z(grid, w_qkv, vectors)
    by_core, by_x = grid.over_core(tokens), grid.over_x(tokens)
    column_one, by_x = lax.optimization_barrier((column_one, by_x))
    near_one = gather_near(grid, column_one)
    column_two = gather_z(grid, after(jnp.concatenate([w_out, w_fc1], axis=1), column_one, by_x))
    near_one = lax.optimization_barrier(near_one)
    far_one = gather_far(grid, *near_one)
    seen = lax.optimization_barrier(jnp.stack([tokens, by_core, by_x, grid.over_core(by_x)]))
    full_qkv, vectors = assemble(grid, (w_qkv.shape[1], LANES), column_one, near_one, far_one)
    column_two = after(column_two, far_one)
    near_two = gather_near(grid, column_two)
    column_three = gather_z(grid, after(w_fc2, column_two))
    near_two = lax.optimization_barrier(near_two)
    far_two = gather_far(grid, *near_two)

    vectors = unfold(vectors, depth_rows, total_len)
    vectors = [v.astype(F32) for v in split_vectors(vectors, lengths)]
    bias_q, bias_v, bias_out, bias_fc1, bias_fc2, gain_one, shift_one, gain_two, shift_two = vectors
    spot = lax.axis_index("seq")
    blocks = grid.seq
    mask_blocks = token_mask.reshape(slots, blocks, local_len)
    keep = jnp.stack([pick(mask_blocks, spot ^ block, 1) for block in range(blocks)], 1)
    valid = (keep[:, 0] > 0).reshape(-1, 1).astype(F32)
    keep = keep.reshape(slots, 1, -1)

    rows = tokens.reshape(-1, width).astype(F32)
    normal_seen, _ = normalise(seen.reshape(-1, width).astype(F32))
    normed_seen = lax.optimization_barrier((normal_seen * gain_one + shift_one).astype(BF16))
    normed_low = normed_seen[:count]
    qkv_bias = jnp.concatenate([bias_q, jnp.zeros_like(bias_out), bias_v])
    projected = (jnp.dot(normed_seen, full_qkv, preferred_element_type=F32) + qkv_bias).astype(BF16)
    projected = projected.reshape(blocks, slots, local_len, 3 * width)

    column_three = after(column_three, far_two, projected)
    near_three = gather_near(grid, column_three)
    full_out, full_fc1 = assemble(grid, (width, w_fc1.shape[1]), column_two, near_two, far_two)
    attended, logs = zip(*[attend_forward(slot, projected, keep) for slot in range(slots)])
    near_three = after(near_three, attended)
    far_three = gather_far(grid, *near_three)
    (full_fc2,) = assemble(grid, (width,), column_three, near_three, far_three)

    attended = jnp.concatenate(attended).reshape(-1, width)
    middle = rows + jnp.dot(attended, full_out, preferred_element_type=F32) + bias_out
    normal_two, scale_two = normalise(middle)
    second_low = (normal_two * gain_two + shift_two).astype(BF16)
    hidden = jnp.dot(second_low, full_fc1, preferred_element_type=F32) + bias_fc1
    below = 0.5 * (1.0 + lax.erf(hidden * math.sqrt(0.5)))
    density = jnp.exp(-0.5 * hidden * hidden) * (1.0 / math.sqrt(2.0 * math.pi))
    activated_low = (hidden * below).astype(BF16)
    slope = (below + hidden * density).astype(BF16)
    activated_low, slope = lax.optimization_barrier((activated_low, slope))

    grad_y_low = cotangent.reshape(-1, width) * valid.astype(BF16)
    grad_y = grad_y_low.astype(F32)
    terms_fc2 = dot_columns(activated_low, grad_y_low).astype(BF16)
    sum_fc2 = reduce_core(grid, terms_fc2)
    grad_y_next, full_fc2 = after((grad_y_low, full_fc2), terms_fc2)
    grad_hidden = (dot_rows(grad_y_next, full_fc2) * slope.astype(F32)).astype(BF16)
    grad_hidden, sum_fc2 = lax.optimization_barrier((grad_hidden, sum_fc2))
    far_fc2 = reduce_far(grid, sum_fc2, 2)
    result = (
        middle + jnp.dot(activated_low, full_fc2, preferred_element_type=F32) + bias_fc2
    ) * valid
    out_tokens = result.astype(BF16).reshape(slots, local_len, width)
    grad_b_fc2 = jnp.sum(grad_y, axis=0)
    terms_fc1 = dot_columns(second_low, grad_hidden).astype(BF16)
    grad_b_fc1 = jnp.sum(grad_hidden.astype(F32), axis=0)
    grad_second = dot_rows(after(grad_hidden, terms_fc1), full_fc1)
    grad_middle, grad_gain_two, grad_shift_two = normalise_back(
        grad_second, gain_two, normal_two, scale_two
    )
    grad_middle = grad_y + grad_middle
    grad_branch = after(grad_middle.astype(BF16), far_fc2)
    near_fc2 = reduce_near(grid, sum_fc2, far_fc2)
    grad_b_out = jnp.sum(grad_branch.astype(F32), axis=0)
    terms_out = dot_columns(attended, grad_branch).astype(BF16)
    sum_two = jnp.concatenate([reduce_core(grid, terms_out), reduce_core(grid, terms_fc1)], axis=-1)
    grad_attended = dot_rows(grad_branch, full_out).astype(BF16).reshape(slots, local_len, width)

    parts, ahead = [], sum_two
    for slot in range(slots):
        grad_attended = after(grad_attended, ahead)
        grad_queries, own, send = attend_backward(slot, projected, keep, logs[slot], grad_attended)
        came = grid.over_core(send)
        across = add(own[1], came[1])
        ahead = (grad_queries, across) if slot == 0 else (grad_queries, across, parts[-1][3])
        if slot == 0:
            near_fc2 = after(near_fc2, grad_queries)
            far_two = reduce_far(grid, after(sum_two, near_fc2), 0)
            grad_w_fc2 = reduce_z(grid, sum_fc2, near_fc2)
            ahead = (grad_queries,)
        else:
            ahead = (grad_queries, parts[-1][4])
        parts.append((grad_queries, own[0], came[0], grid.over_x(across), across))
    near_two = reduce_near(grid, sum_two, far_two)
    grad_two = reduce_z(grid, sum_two, near_two)
    grad_w_out, grad_w_fc1 = grad_two[:, :width], grad_two[:, width:]

    grad_queries = jnp.concatenate([part[0] for part in parts]).reshape(-1, width)
    terms_q = dot_columns(normed_low, grad_queries).astype(BF16)
    sum_q = reduce_core(grid, terms_q)
    far_q = reduce_far(grid, sum_q, 0)
    grad_keys_values = [
        (own.astype(F32) + came.astype(F32) + across.astype(F32)).astype(BF16)
        for _, own, came, across, _ in parts
    ]
    grad_keys, grad_values = [jnp.stack([part[kind] for part in grad_keys_values]) for kind in range(2)]
    grad_kv = jnp.concatenate([grad_keys, grad_values], axis=-1).reshape(-1, 2 * width)
    grad_kv, grad_w_fc2 = lax.optimization_barrier((grad_kv, grad_w_fc2))
    terms_kv = dot_columns(normed_low, grad_kv).astype(BF16)
    sum_kv = reduce_core(grid, terms_kv)
    far_kv = reduce_far(grid, sum_kv, 2)
    grad_qkv = after(jnp.concatenate([grad_queries, grad_kv], axis=-1), terms_kv)
    grad_normed = dot_rows(grad_qkv, full_qkv)
    grad_qkv_wide = jnp.sum(grad_qkv.astype(F32), axis=0)
    grad_b_q = grad_qkv_wide[:width]
    grad_b_v = grad_qkv_wide[2 * width :]
    normal_one, scale_one = normalise(rows)
    grad_rows, grad_gain_one, grad_shift_one = normalise_back(
        grad_normed, gain_one, normal_one, scale_one
    )
    grad_tokens = (grad_middle + grad_rows).reshape(slots, local_len, width)
    terms = (
        grad_b_q,
        grad_b_v,
        grad_b_out,
        grad_b_fc1,
        grad_b_fc2,
        grad_gain_one,
        grad_shift_one,
        grad_gain_two,
        grad_shift_two,
    )
    terms = jnp.concatenate([term.reshape(groups, -1) for term in terms], axis=-1)
    owned = split_vectors(reduce_small(grid, terms[:, None]).reshape(1, -1), lengths)
    near_q = reduce_near(grid, sum_q, far_q)
    near_kv = reduce_near(grid, sum_kv, far_kv)
    grad_w_qkv = jnp.concatenate([reduce_z(grid, sum_q, near_q), reduce_z(grid, sum_kv, near_kv)], axis=-1)
    return (out_tokens, grad_tokens, grad_w_qkv, grad_w_out, grad_w_fc1, grad_w_fc2, *owned)


def solution(mesh):
    spread = P(("dp", "seq"))
    row = P("dp", "seq", None)
    matrix = P(("dp", "seq"), None)
    in_specs = (row, row, P("dp", None)) + (matrix,) * 4 + (spread,) * 9
    out_specs = (row, row) + (matrix,) * 4 + (spread,) * 9
    return jax.shard_map(shards, mesh=mesh, in_specs=in_specs, out_specs=out_specs, check_vma=False)
```
